32 devices in a mesh: win: 2 (over y), tile: 4 (over x, core), chan: 4 (over z).
Axes of the slice: x: 2, y: 2, z: 4, core: 2. Of those that a mesh axis runs over, the one named last changes fastest.
Arguments:
- residual: float32 [32, 128, 2048], P(('win', 'tile', 'chan')), parts along dimension 0, may hold values from -6 to 6
- freq_index: int32 [32], P('win'), parts along dimension 0, may hold values from 0 to 1023, as said below
- psf_profile: float32 [32, 2, 257], P(('win', 'tile', 'chan')), parts along dimension 0, may hold values from -0.3 to 0.3
Outputs:
- taylor_step: float32 [3, 256, 2048], P(None, ('win', 'tile'), 'chan'), parts along dimension 1
- new_residual: float32 [32, 128, 2048], P(('win', 'tile', 'chan')), parts along dimension 0
The draws below stay inside these ranges and needn't reach their ends.
There are 2 independent parts, one for each index of `win`. The reference program is written for one: setup_inputs(seed, part) draws one part's arguments, and reference() takes and returns one part's arrays. A program takes and returns all parts, laid end to end along the dimension named above; each array names one. Nothing has to cross between parts.
Inputs may be any that keep to these rules, and one draw needn't show every extreme that they name: `freq_index`: the values are distinct, and both ends of the grid, 0 and 1023, occur.
All inputs are finite; a program needn't handle non-finite values.
Results may differ from the reference program's by a relative error of at most 0.00013.
Values sent between devices are 32-bit elements; how exact they have to be, the bound alone decides.
A program may use at most 64 MiB of HBM per device.

```python
import jax
import jax.numpy as jnp
from jax import lax

C = 16
FREQS = 1024
H = 128
W = 2048
K = 128


def draw_freq_index(key, part):
    key = jax.random.fold_in(key, 7)
    first_key, second_key = jax.random.split(key)
    middle = jax.random.permutation(first_key, FREQS - 2)[:C - 2] + 1
    values = jnp.concatenate([jnp.array([0, FREQS - 1], jnp.int32), middle.astype(jnp.int32)])
    return jax.random.permutation(second_key, values)


def shard_levels(key, dims, cuts, smallest, top_value):
    def one(dim, shards_of):
        heights = jax.random.uniform(jax.random.fold_in(jax.random.fold_in(key, 6), dim), (shards_of,), jnp.float32, smallest / len(cuts), top_value / len(cuts))
        return jnp.repeat(jnp.exp(heights), dims[dim] // shards_of).reshape((-1,) + (1,) * (len(dims) - dim - 1))

    gain = one(*cuts[0])
    for cut in cuts[1:]:
        gain = gain * one(*cut)
    return gain


def noise(rng, dims, deviation, limit, cuts=(), kind=jnp.bfloat16):
    factor_of = shard_levels(rng, dims, cuts, -0.22, 0.18) if cuts else 1.0
    values = jax.random.normal(rng, dims, jnp.float32) * deviation * factor_of
    return jnp.minimum(jnp.maximum(values, -limit), limit).astype(kind)


def setup_inputs(seed: int = 0, part: int = 0) -> dict:
    seeds = jax.random.split(jax.random.key(seed), 4)
    part_keys = jax.random.split(jax.random.fold_in(seeds[3], part), 4)
    return {
        "residual": noise(part_keys[0], (C, H, W), 1.0, 6.0, ((0, 16),), jnp.float32),
        "freq_index": draw_freq_index(jax.random.fold_in(jax.random.fold_in(seeds[3], part), 71), part),
        "psf_profile": jnp.clip(jax.random.uniform(part_keys[2], (C, 2, 2 * K + 1), jnp.float32, -0.3, 0.3) * shard_levels(part_keys[2], (C, 2, 2 * K + 1), ((0, 16),), -0.4, 0.0), -0.3, 0.3),
    }


highest = lax.Precision.HIGHEST


def spectral_weights(freq_index):
    offset = 2.0 * freq_index.astype(jnp.float32) / (FREQS - 1) - 1.0
    return jnp.stack([jnp.ones_like(offset), offset, offset * offset])


def inverse_three(matrix):
    first_row, second_row, third_row = matrix[0], matrix[1], matrix[2]
    cross_one = jnp.cross(second_row, third_row)
    cross_two = jnp.cross(third_row, first_row)
    cross_three = jnp.cross(first_row, second_row)
    determinant = jnp.sum(first_row * cross_one)
    return jnp.stack([cross_one, cross_two, cross_three], axis=1) / determinant


def band_blocks(profile):
    half_width = (profile.shape[0] - 1) // 2
    extended = jnp.pad(profile, (383 - half_width, 383 - half_width))
    blocks = []
    for shift in (-1, 0, 1):
        window = extended[128 * shift + 256:128 * shift + 511][::-1]
        padded = jnp.concatenate([window, jnp.zeros((1,), window.dtype)])
        tiled = jnp.tile(padded, 128)
        skewed = tiled[127:127 + 128 * 255].reshape(128, 255)[:, :128]
        blocks.append(skewed)
    return jnp.stack(blocks)


def along_last(field, blocks):
    count = field.shape[-1] // 128
    shaped = field.reshape(field.shape[:-1] + (count, 128))
    padded = jnp.pad(shaped, [(0, 0)] * (field.ndim - 1) + [(1, 1), (0, 0)])
    result = jnp.einsum("...bi,io->...bo", padded[..., 0:count, :], blocks[0], precision=highest)
    result = result + jnp.einsum("...bi,io->...bo", padded[..., 1:count + 1, :], blocks[1], precision=highest)
    result = result + jnp.einsum("...bi,io->...bo", padded[..., 2:count + 2, :], blocks[2], precision=highest)
    return result.reshape(field.shape)


def along_first(field, blocks):
    count = field.shape[0] // 128
    shaped = field.reshape((count, 128, field.shape[1]))
    padded = jnp.pad(shaped, [(1, 1), (0, 0), (0, 0)])
    result = jnp.einsum("biw,io->bow", padded[0:count], blocks[0], precision=highest)
    result = result + jnp.einsum("biw,io->bow", padded[1:count + 1], blocks[1], precision=highest)
    result = result + jnp.einsum("biw,io->bow", padded[2:count + 2], blocks[2], precision=highest)
    return result.reshape(field.shape)


def reference(residual, freq_index, psf_profile):
    weights = spectral_weights(freq_index)
    hessian = jnp.dot(weights, weights.T, precision=highest)
    solver = inverse_three(hessian)
    gradient = jnp.einsum("tc,chw->thw", weights, residual, precision=highest)
    taylor_step = jnp.einsum("ts,shw->thw", solver, gradient, precision=highest)

    def update(items):
        plane, channel_weights, profile = items
        model = jnp.einsum("t,thw->hw", channel_weights, taylor_step, precision=highest)
        rowwise = along_last(model, band_blocks(profile[1]))
        blurred = along_first(rowwise, band_blocks(profile[0]))
        return plane - blurred

    new_residual = lax.map(update, (residual, weights.T, psf_profile))
    return taylor_step, new_residual
```

```python
import functools

import jax
import jax.numpy as jnp
from jax import lax
from jax.experimental import pallas as pl
from jax.experimental.pallas import tpu as pltpu
from jax.sharding import PartitionSpec as P

FREQS = 1024
MESH = pl.DeviceIdType.MESH
HOP = 2
CHUNK = 256


def split_halves(x):
    high = x.astype(jnp.bfloat16)
    low = (x - high.astype(jnp.float32)).astype(jnp.bfloat16)
    return high, low


def dot_split(a, b, dims):
    def one(x, y):
        return lax.dot_general(x, y, (dims, ((), ())), preferred_element_type=jnp.float32)

    return one(a[0], b[0]) + (one(a[0], b[1]) + one(a[1], b[0]))


def kernel(
    tiles, depth, chunks, res, freq, psf, taylor_out, new_out,
    raw, part, left_in, right_in, left_sum, right_sum, steps, outgoing, model,
    profile, row_high, row_low, col_high, col_low, weight_s,
    raw_send, raw_recv, mod_send, mod_recv, rt_send, rt_recv, lf_send, lf_recv,
):
    a = lax.axis_index("tile")
    k = lax.axis_index("chan")
    height = res.shape[1]
    rows = height // tiles
    total = freq.shape[0]

    def member(d):
        return lax.rem(a + d, tiles)

    barrier = pltpu.get_barrier_semaphore()
    for d in range(1, tiles):
        pl.semaphore_signal(barrier, inc=1, device_id={"tile": member(d)}, device_id_type=MESH)

    @pl.when(k > 0)
    def _():
        pl.semaphore_signal(barrier, inc=1, device_id={"chan": k - 1}, device_id_type=MESH)

    @pl.when(k < depth - 1)
    def _():
        pl.semaphore_signal(barrier, inc=1, device_id={"chan": k + 1}, device_id_type=MESH)

    ends = jnp.where(k > 0, 1, 0) + jnp.where(k < depth - 1, 1, 0)
    pl.semaphore_wait(barrier, tiles - 1 + ends)

    def own_rows(b):
        return pl.ds(pl.multiple_of(b * rows, rows), rows)

    def columns(j):
        return pl.ds(pl.multiple_of(j * CHUNK, CHUNK), CHUNK)

    def raw_copy(j, d):
        return pltpu.make_async_remote_copy(
            src_ref=res.at[0, own_rows(member(d)), columns(j)],
            dst_ref=raw.at[j, d - 1],
            send_sem=raw_send.at[j, d - 1],
            recv_sem=raw_recv.at[j, d - 1],
            device_id={"tile": member(d)},
            device_id_type=MESH,
        )

    def model_copy(j, d):
        return pltpu.make_async_remote_copy(
            src_ref=outgoing.at[j, d - 1],
            dst_ref=model.at[j + 1, own_rows(a)],
            send_sem=mod_send.at[j, d - 1],
            recv_sem=mod_recv.at[j, d - 1],
            device_id={"tile": member(d)},
            device_id_type=MESH,
        )

    def right_copy(j):
        return pltpu.make_async_remote_copy(
            src_ref=left_sum.at[j], dst_ref=left_in.at[j],
            send_sem=rt_send.at[j], recv_sem=rt_recv.at[j],
            device_id={"chan": lax.rem(k + 1, depth)}, device_id_type=MESH,
        )

    def left_copy(j):
        return pltpu.make_async_remote_copy(
            src_ref=right_sum.at[j], dst_ref=right_in.at[j],
            send_sem=lf_send.at[j], recv_sem=lf_recv.at[j],
            device_id={"chan": lax.rem(k + depth - 1, depth)}, device_id_type=MESH,
        )

    def send_raw(j, carry):
        for d in range(1, tiles):
            raw_copy(j, d).start()
        return carry

    lax.fori_loop(0, chunks, send_raw, 0)

    def offset_of(c):
        return 2.0 * freq[c].astype(jnp.float32) / (FREQS - 1) - 1.0

    def add_powers(c, sums):
        x = offset_of(c)
        y = x * x
        return sums[0] + x, sums[1] + y, sums[2] + x * y, sums[3] + y * y

    zero = jnp.float32(0.0)
    s1, s2, s3, s4 = lax.fori_loop(0, total, add_powers, (zero, zero, zero, zero))
    m = ((jnp.float32(total), s1, s2), (s1, s2, s3), (s2, s3, s4))

    def cross(p, q):
        return (p[1] * q[2] - p[2] * q[1], p[2] * q[0] - p[0] * q[2], p[0] * q[1] - p[1] * q[0])

    crosses = (cross(m[1], m[2]), cross(m[2], m[0]), cross(m[0], m[1]))
    det = m[0][0] * crosses[0][0] + m[0][1] * crosses[0][1] + m[0][2] * crosses[0][2]
    for t in range(3):
        for s in range(3):
            weight_s[2 * tiles + 3 * t + s] = crosses[s][t] / det
    for d in range(tiles):
        x = offset_of(member(d) * depth + k)
        weight_s[2 * d] = x
        weight_s[2 * d + 1] = x * x

    profile[...] = jnp.zeros_like(profile)
    profile[:, 0 : psf.shape[2]] = psf[0]
    wide = profile.shape[1]
    band = pltpu.roll(
        jnp.broadcast_to(profile[1:2, :], (CHUNK, wide)), 0, 1, stride=1, stride_axis=0
    )
    row_high[...], row_low[...] = split_halves(band)
    half = (psf.shape[2] - 1) // 2
    band = pltpu.roll(
        jnp.broadcast_to(profile[0:1, :], (height, wide)), wide - half, 1, stride=1, stride_axis=0
    )[:, :height]
    col_high[...], col_low[...] = split_halves(band)
    model[0] = jnp.zeros(model.shape[1:], jnp.float32)
    model[chunks + 1] = jnp.zeros(model.shape[1:], jnp.float32)

    lag_left = HOP * k
    lag_right = HOP * (depth - 1 - k)
    lag = jnp.maximum(lag_left, lag_right)

    def inside(j):
        return jnp.logical_and(j >= 0, j < chunks)

    def step(s, carry):
        @pl.when(s < chunks)
        def _():
            j = s
            own = res[0, own_rows(a), columns(j)]
            sums = [own, own * weight_s[0], own * weight_s[1]]
            for d in range(1, tiles):
                raw_copy(j, d).wait_recv()
            for d in range(1, tiles):
                e = tiles - d
                piece = raw[j, d - 1]
                sums[0] += piece
                sums[1] += piece * weight_s[2 * e]
                sums[2] += piece * weight_s[2 * e + 1]
            for t in range(3):
                part[j, t] = sums[t]

        jl = s - lag_left

        @pl.when(inside(jl))
        def _():
            @pl.when(k == 0)
            def _():
                left_sum[jl] = part[jl]

            @pl.when(k > 0)
            def _():
                right_copy(jl).wait_recv()
                left_sum[jl] = left_in[jl] + part[jl]

            @pl.when(k < depth - 1)
            def _():
                right_copy(jl).start()

        jr = s - lag_right

        @pl.when(inside(jr))
        def _():
            @pl.when(k == depth - 1)
            def _():
                right_sum[jr] = part[jr]

            @pl.when(k < depth - 1)
            def _():
                left_copy(jr).wait_recv()
                right_sum[jr] = right_in[jr] + part[jr]

            @pl.when(k > 0)
            def _():
                left_copy(jr).start()

        jt = s - lag

        @pl.when(inside(jt))
        def _():
            @pl.when(k == 0)
            def _():
                steps[jt] = right_sum[jt]

            @pl.when(k > 0)
            def _():
                steps[jt] = left_in[jt] + right_sum[jt]

            g = [steps[jt, t] for t in range(3)]
            base = 2 * tiles
            u = [
                weight_s[base + 3 * t] * g[0]
                + weight_s[base + 3 * t + 1] * g[1]
                + weight_s[base + 3 * t + 2] * g[2]
                for t in range(3)
            ]
            for t in range(3):
                steps[jt, t] = u[t]
            for d in range(1, tiles):
                outgoing[jt, d - 1] = u[0] + weight_s[2 * d] * u[1] + weight_s[2 * d + 1] * u[2]
                model_copy(jt, d).start()
            model[jt + 1, own_rows(a)] = u[0] + weight_s[0] * u[1] + weight_s[1] * u[2]

        jb = jt - 1

        @pl.when(jnp.logical_and(jb + 1 >= 0, jb + 1 < chunks))
        def _():
            for d in range(1, tiles):
                model_copy(jb + 1, d).wait_recv()

        @pl.when(inside(jb))
        def _():
            field = jnp.concatenate(
                [model[jb, :, CHUNK - half :], model[jb + 1], model[jb + 2, :, :half]], axis=1
            )
            rowwise = dot_split(split_halves(field), (row_high[...], row_low[...]), ((1,), (1,)))
            blurred = dot_split((col_high[...], col_low[...]), split_halves(rowwise), ((1,), (0,)))
            new_out[0, :, columns(jb)] = res[0, :, columns(jb)] - blurred

        return carry

    lax.fori_loop(0, chunks + HOP * (depth - 1) + 1, step, 0)

    per = taylor_out.shape[2] // CHUNK
    for i in range(per):
        taylor_out[:, :, i * CHUNK : (i + 1) * CHUNK] = steps[k * per + i]

    def drain(j, carry):
        for d in range(1, tiles):
            raw_copy(j, d).wait_send()
            model_copy(j, d).wait_send()

        @pl.when(k < depth - 1)
        def _():
            right_copy(j).wait_send()

        @pl.when(k > 0)
        def _():
            left_copy(j).wait_send()

        return carry

    lax.fori_loop(0, chunks, drain, 0)


def solution(mesh):
    tiles, depth = mesh.shape["tile"], mesh.shape["chan"]

    def shards(residual, freq_index, psf_profile):
        _, height, width = residual.shape
        rows, block = height // tiles, width // depth
        chunks = width // CHUNK
        half = (psf_profile.shape[2] - 1) // 2
        f32, bf16 = jnp.float32, jnp.bfloat16
        chain = pltpu.VMEM((chunks, 3, rows, CHUNK), f32)
        vmem = pl.BlockSpec(memory_space=pltpu.VMEM)
        dma = pltpu.SemaphoreType.DMA
        return pl.pallas_call(
            functools.partial(kernel, tiles, depth, chunks),
            out_shape=(
                jax.ShapeDtypeStruct((3, rows, block), f32),
                jax.ShapeDtypeStruct(residual.shape, f32),
            ),
            in_specs=[vmem, pl.BlockSpec(memory_space=pltpu.SMEM), vmem],
            out_specs=(vmem, vmem),
            scratch_shapes=[
                pltpu.VMEM((chunks, tiles - 1, rows, CHUNK), f32),
                chain, chain, chain, chain, chain, chain,
                pltpu.VMEM((chunks, tiles - 1, rows, CHUNK), f32),
                pltpu.VMEM((chunks + 2, height, CHUNK), f32),
                pltpu.VMEM((2, CHUNK + 2 * half), f32),
                pltpu.VMEM((CHUNK, CHUNK + 2 * half), bf16),
                pltpu.VMEM((CHUNK, CHUNK + 2 * half), bf16),
                pltpu.VMEM((height, height), bf16),
                pltpu.VMEM((height, height), bf16),
                pltpu.SMEM((2 * tiles + 9,), f32),
                dma((chunks, tiles - 1)), dma((chunks, tiles - 1)),
                dma((chunks, tiles - 1)), dma((chunks, tiles - 1)),
                dma((chunks,)), dma((chunks,)), dma((chunks,)), dma((chunks,)),
            ],
            compiler_params=pltpu.CompilerParams(
                collective_id=0, has_side_effects=True, vmem_limit_bytes=40 * 1024 * 1024
            ),
        )(residual, freq_index, psf_profile)

    in_specs = (
        P(("win", "tile", "chan"), None, None),
        P("win"),
        P(("win", "tile", "chan"), None, None),
    )
    out_specs = (P(None, ("win", "tile"), "chan"), P(("win", "tile", "chan"), None, None))
    return jax.shard_map(shards, mesh=mesh, in_specs=in_specs, out_specs=out_specs, check_vma=False)
```

```python
import functools

import jax
import jax.numpy as jnp
from jax import lax
from jax.experimental import pallas as pl
from jax.experimental.pallas import tpu as pltpu
from jax.sharding import PartitionSpec as P

FREQS = 1024
MESH = pl.DeviceIdType.MESH
HOP = 2
BACK = 3
CHUNK = 256


def split_halves(x):
    high = x.astype(jnp.bfloat16)
    low = (x - high.astype(jnp.float32)).astype(jnp.bfloat16)
    return high, low


def dot_split(a, b, dims):
    def one(x, y):
        return lax.dot_general(x, y, (dims, ((), ())), preferred_element_type=jnp.float32)

    return one(a[0], b[0]) + (one(a[0], b[1]) + one(a[1], b[0]))


def kernel(
    tiles, depth, chunks, res, freq, psf, taylor_out, new_out,
    raw, part, left_in, right_in, left_sum, right_sum, steps, outgoing, model,
    profile, row_high, row_low, col_high, col_low, weight_s,
    raw_send, raw_recv, mod_send, mod_recv, rt_send, rt_recv, lf_send, lf_recv,
):
    a = lax.axis_index("tile")
    k = lax.axis_index("chan")
    height = res.shape[1]
    rows = height // tiles
    total = freq.shape[0]

    def member(d):
        return lax.rem(a + d, tiles)

    barrier = pltpu.get_barrier_semaphore()
    for d in range(1, tiles):
        pl.semaphore_signal(barrier, inc=1, device_id={"tile": member(d)}, device_id_type=MESH)

    @pl.when(k > 0)
    def _():
        pl.semaphore_signal(barrier, inc=1, device_id={"chan": k - 1}, device_id_type=MESH)

    @pl.when(k < depth - 1)
    def _():
        pl.semaphore_signal(barrier, inc=1, device_id={"chan": k + 1}, device_id_type=MESH)

    ends = jnp.where(k > 0, 1, 0) + jnp.where(k < depth - 1, 1, 0)
    pl.semaphore_wait(barrier, tiles - 1 + ends)

    def own_rows(b):
        return pl.ds(pl.multiple_of(b * rows, rows), rows)

    def columns(j):
        return pl.ds(pl.multiple_of(j * CHUNK, CHUNK), CHUNK)

    def raw_copy(j, d):
        return pltpu.make_async_remote_copy(
            src_ref=res.at[0, own_rows(member(d)), columns(j)],
            dst_ref=raw.at[j, d - 1],
            send_sem=raw_send.at[j, d - 1],
            recv_sem=raw_recv.at[j, d - 1],
            device_id={"tile": member(d)},
            device_id_type=MESH,
        )

    def model_copy(j, d):
        return pltpu.make_async_remote_copy(
            src_ref=outgoing.at[j, d - 1],
            dst_ref=model.at[j + 1, own_rows(a)],
            send_sem=mod_send.at[j, d - 1],
            recv_sem=mod_recv.at[j, d - 1],
            device_id={"tile": member(d)},
            device_id_type=MESH,
        )

    def right_copy(j):
        return pltpu.make_async_remote_copy(
            src_ref=left_sum.at[j], dst_ref=left_in.at[j],
            send_sem=rt_send.at[j], recv_sem=rt_recv.at[j],
            device_id={"chan": lax.rem(k + 1, depth)}, device_id_type=MESH,
        )

    def left_copy(j):
        return pltpu.make_async_remote_copy(
            src_ref=right_sum.at[j], dst_ref=right_in.at[j],
            send_sem=lf_send.at[j], recv_sem=lf_recv.at[j],
            device_id={"chan": lax.rem(k + depth - 1, depth)}, device_id_type=MESH,
        )

    def send_raw(j, carry):
        for d in range(1, tiles):
            raw_copy(j, d).start()
        return carry

    lax.fori_loop(0, chunks, send_raw, 0)

    def offset_of(c):
        return 2.0 * freq[c].astype(jnp.float32) / (FREQS - 1) - 1.0

    def add_powers(c, sums):
        x = offset_of(c)
        y = x * x
        return sums[0] + x, sums[1] + y, sums[2] + x * y, sums[3] + y * y

    zero = jnp.float32(0.0)
    s1, s2, s3, s4 = lax.fori_loop(0, total, add_powers, (zero, zero, zero, zero))
    m = ((jnp.float32(total), s1, s2), (s1, s2, s3), (s2, s3, s4))

    def cross(p, q):
        return (p[1] * q[2] - p[2] * q[1], p[2] * q[0] - p[0] * q[2], p[0] * q[1] - p[1] * q[0])

    crosses = (cross(m[1], m[2]), cross(m[2], m[0]), cross(m[0], m[1]))
    det = m[0][0] * crosses[0][0] + m[0][1] * crosses[0][1] + m[0][2] * crosses[0][2]
    for t in range(3):
        for s in range(3):
            weight_s[2 * tiles + 3 * t + s] = crosses[s][t] / det
    for d in range(tiles):
        x = offset_of(member(d) * depth + k)
        weight_s[2 * d] = x
        weight_s[2 * d + 1] = x * x

    profile[...] = jnp.zeros_like(profile)
    profile[:, 0 : psf.shape[2]] = psf[0]
    wide = profile.shape[1]
    band = pltpu.roll(
        jnp.broadcast_to(profile[1:2, :], (CHUNK, wide)), 0, 1, stride=1, stride_axis=0
    )
    row_high[...], row_low[...] = split_halves(band)
    half = (psf.shape[2] - 1) // 2
    band = pltpu.roll(
        jnp.broadcast_to(profile[0:1, :], (height, wide)), wide - half, 1, stride=1, stride_axis=0
    )[:, :height]
    col_high[...], col_low[...] = split_halves(band)
    model[0] = jnp.zeros(model.shape[1:], jnp.float32)
    model[chunks + 1] = jnp.zeros(model.shape[1:], jnp.float32)

    lag_left = HOP * k
    lag_right = HOP * (depth - 1 - k)
    lag = jnp.maximum(lag_left, lag_right)

    def inside(j):
        return jnp.logical_and(j >= 0, j < chunks)

    def step(s, carry):
        @pl.when(s < chunks)
        def _():
            j = s
            own = res[0, own_rows(a), columns(j)]
            sums = [own, own * weight_s[0], own * weight_s[1]]
            for d in range(1, tiles):
                raw_copy(j, d).wait_recv()
            for d in range(1, tiles):
                e = tiles - d
                piece = raw[j, d - 1]
                sums[0] += piece
                sums[1] += piece * weight_s[2 * e]
                sums[2] += piece * weight_s[2 * e + 1]
            for t in range(3):
                part[j, t] = sums[t]

        jl = s - lag_left

        @pl.when(inside(jl))
        def _():
            @pl.when(k == 0)
            def _():
                left_sum[jl] = part[jl]

            @pl.when(k > 0)
            def _():
                right_copy(jl).wait_recv()
                left_sum[jl] = left_in[jl] + part[jl]

            @pl.when(k < depth - 1)
            def _():
                right_copy(jl).start()

        jr = s - lag_right

        @pl.when(inside(jr))
        def _():
            @pl.when(k == depth - 1)
            def _():
                right_sum[jr] = part[jr]

            @pl.when(k < depth - 1)
            def _():
                left_copy(jr).wait_recv()
                right_sum[jr] = right_in[jr] + part[jr]

            @pl.when(k > 0)
            def _():
                left_copy(jr).start()

        jt = s - lag

        @pl.when(inside(jt))
        def _():
            @pl.when(k == 0)
            def _():
                steps[jt] = right_sum[jt]

            @pl.when(k > 0)
            def _():
                steps[jt] = left_in[jt] + right_sum[jt]

            g = [steps[jt, t] for t in range(3)]
            base = 2 * tiles
            u = [
                weight_s[base + 3 * t] * g[0]
                + weight_s[base + 3 * t + 1] * g[1]
                + weight_s[base + 3 * t + 2] * g[2]
                for t in range(3)
            ]
            for t in range(3):
                steps[jt, t] = u[t]
            for d in range(1, tiles):
                outgoing[jt, d - 1] = u[0] + weight_s[2 * d] * u[1] + weight_s[2 * d + 1] * u[2]
                model_copy(jt, d).start()
            model[jt + 1, own_rows(a)] = u[0] + weight_s[0] * u[1] + weight_s[1] * u[2]

        jb = jt - BACK

        @pl.when(jnp.logical_and(jb + 1 >= 0, jb + 1 < chunks))
        def _():
            for d in range(1, tiles):
                model_copy(jb + 1, d).wait_recv()

        @pl.when(inside(jb))
        def _():
            field = jnp.concatenate(
                [model[jb, :, CHUNK - half :], model[jb + 1], model[jb + 2, :, :half]], axis=1
            )
            rowwise = dot_split(split_halves(field), (row_high[...], row_low[...]), ((1,), (1,)))
            blurred = dot_split((col_high[...], col_low[...]), split_halves(rowwise), ((1,), (0,)))
            new_out[0, :, columns(jb)] = res[0, :, columns(jb)] - blurred

        return carry

    lax.fori_loop(0, chunks + HOP * (depth - 1) + BACK, step, 0)

    per = taylor_out.shape[2] // CHUNK
    for i in range(per):
        taylor_out[:, :, i * CHUNK : (i + 1) * CHUNK] = steps[k * per + i]

    def drain(j, carry):
        for d in range(1, tiles):
            raw_copy(j, d).wait_send()
            model_copy(j, d).wait_send()

        @pl.when(k < depth - 1)
        def _():
            right_copy(j).wait_send()

        @pl.when(k > 0)
        def _():
            left_copy(j).wait_send()

        return carry

    lax.fori_loop(0, chunks, drain, 0)


def solution(mesh):
    tiles, depth = mesh.shape["tile"], mesh.shape["chan"]

    def shards(residual, freq_index, psf_profile):
        _, height, width = residual.shape
        rows, block = height // tiles, width // depth
        chunks = width // CHUNK
        half = (psf_profile.shape[2] - 1) // 2
        f32, bf16 = jnp.float32, jnp.bfloat16
        chain = pltpu.VMEM((chunks, 3, rows, CHUNK), f32)
        vmem = pl.BlockSpec(memory_space=pltpu.VMEM)
        dma = pltpu.SemaphoreType.DMA
        return pl.pallas_call(
            functools.partial(kernel, tiles, depth, chunks),
            out_shape=(
                jax.ShapeDtypeStruct((3, rows, block), f32),
                jax.ShapeDtypeStruct(residual.shape, f32),
            ),
            in_specs=[vmem, pl.BlockSpec(memory_space=pltpu.SMEM), vmem],
            out_specs=(vmem, vmem),
            scratch_shapes=[
                pltpu.VMEM((chunks, tiles - 1, rows, CHUNK), f32),
                chain, chain, chain, chain, chain, chain,
                pltpu.VMEM((chunks, tiles - 1, rows, CHUNK), f32),
                pltpu.VMEM((chunks + 2, height, CHUNK), f32),
                pltpu.VMEM((2, CHUNK + 2 * half), f32),
                pltpu.VMEM((CHUNK, CHUNK + 2 * half), bf16),
                pltpu.VMEM((CHUNK, CHUNK + 2 * half), bf16),
                pltpu.VMEM((height, height), bf16),
                pltpu.VMEM((height, height), bf16),
                pltpu.SMEM((2 * tiles + 9,), f32),
                dma((chunks, tiles - 1)), dma((chunks, tiles - 1)),
                dma((chunks, tiles - 1)), dma((chunks, tiles - 1)),
                dma((chunks,)), dma((chunks,)), dma((chunks,)), dma((chunks,)),
            ],
            compiler_params=pltpu.CompilerParams(
                collective_id=0, has_side_effects=True, vmem_limit_bytes=40 * 1024 * 1024
            ),
        )(residual, freq_index, psf_profile)

    in_specs = (
        P(("win", "tile", "chan"), None, None),
        P("win"),
        P(("win", "tile", "chan"), None, None),
    )
    out_specs = (P(None, ("win", "tile"), "chan"), P(("win", "tile", "chan"), None, None))
    return jax.shard_map(shards, mesh=mesh, in_specs=in_specs, out_specs=out_specs, check_vma=False)
```

```python
import functools

import jax
import jax.numpy as jnp
from jax import lax
from jax.experimental import pallas as pl
from jax.experimental.pallas import tpu as pltpu
from jax.sharding import PartitionSpec as P

FREQS = 1024
MESH = pl.DeviceIdType.MESH
HOP = 4
BACK = 6
CHUNK = 128


def split_halves(x):
    high = x.astype(jnp.bfloat16)
    low = (x - high.astype(jnp.float32)).astype(jnp.bfloat16)
    return high, low


def dot_split(a, b, dims):
    def one(x, y):
        return lax.dot_general(x, y, (dims, ((), ())), preferred_element_type=jnp.float32)

    return one(a[0], b[0]) + (one(a[0], b[1]) + one(a[1], b[0]))


def kernel(
    tiles, depth, chunks, res_hbm, freq_hbm, psf_hbm, taylor_out, new_out,
    res, freq, psf, result,
    raw, part, left_in, right_in, left_sum, right_sum, steps, outgoing, model,
    profile, row_high, row_low, col_high, col_low, weight_s,
    raw_send, raw_recv, mod_send, mod_recv, rt_send, rt_recv, lf_send, lf_recv,
    local, out_sem, step_sem,
):
    a = lax.axis_index("tile")
    k = lax.axis_index("chan")
    height = res.shape[1]
    rows = height // tiles
    total = freq.shape[0]

    loads = [
        pltpu.make_async_copy(freq_hbm, freq, local.at[0]),
        pltpu.make_async_copy(psf_hbm, psf, local.at[1]),
        pltpu.make_async_copy(res_hbm, res, local.at[2]),
    ]
    for load in loads:
        load.start()

    def member(d):
        return lax.rem(a + d, tiles)

    barrier = pltpu.get_barrier_semaphore()
    for d in range(1, tiles):
        pl.semaphore_signal(barrier, inc=1, device_id={"tile": member(d)}, device_id_type=MESH)

    @pl.when(k > 0)
    def _():
        pl.semaphore_signal(barrier, inc=1, device_id={"chan": k - 1}, device_id_type=MESH)

    @pl.when(k < depth - 1)
    def _():
        pl.semaphore_signal(barrier, inc=1, device_id={"chan": k + 1}, device_id_type=MESH)

    ends = jnp.where(k > 0, 1, 0) + jnp.where(k < depth - 1, 1, 0)
    pl.semaphore_wait(barrier, tiles - 1 + ends)

    def own_rows(b):
        return pl.ds(pl.multiple_of(b * rows, rows), rows)

    def columns(j):
        return pl.ds(pl.multiple_of(j * CHUNK, CHUNK), CHUNK)

    def raw_copy(j, d):
        return pltpu.make_async_remote_copy(
            src_ref=res_hbm.at[0, own_rows(member(d)), columns(j)],
            dst_ref=raw.at[j, d - 1],
            send_sem=raw_send.at[j, d - 1],
            recv_sem=raw_recv.at[j, d - 1],
            device_id={"tile": member(d)},
            device_id_type=MESH,
        )

    def model_copy(j, d):
        return pltpu.make_async_remote_copy(
            src_ref=outgoing.at[j, d - 1],
            dst_ref=model.at[j + 1, own_rows(a)],
            send_sem=mod_send.at[j, d - 1],
            recv_sem=mod_recv.at[j, d - 1],
            device_id={"tile": member(d)},
            device_id_type=MESH,
        )

    def right_copy(j):
        return pltpu.make_async_remote_copy(
            src_ref=left_sum.at[j], dst_ref=left_in.at[j],
            send_sem=rt_send.at[j], recv_sem=rt_recv.at[j],
            device_id={"chan": lax.rem(k + 1, depth)}, device_id_type=MESH,
        )

    def left_copy(j):
        return pltpu.make_async_remote_copy(
            src_ref=right_sum.at[j], dst_ref=right_in.at[j],
            send_sem=lf_send.at[j], recv_sem=lf_recv.at[j],
            device_id={"chan": lax.rem(k + depth - 1, depth)}, device_id_type=MESH,
        )

    def out_copy(j):
        return pltpu.make_async_copy(
            result.at[j], new_out.at[0, :, columns(j)], out_sem.at[j]
        )

    def send_raw(j, carry):
        for d in range(1, tiles):
            raw_copy(j, d).start()
        return carry

    lax.fori_loop(0, chunks, send_raw, 0)

    def offset_of(c):
        return 2.0 * freq[c].astype(jnp.float32) / (FREQS - 1) - 1.0

    def add_powers(c, sums):
        x = offset_of(c)
        y = x * x
        return sums[0] + x, sums[1] + y, sums[2] + x * y, sums[3] + y * y

    loads[0].wait()
    zero = jnp.float32(0.0)
    s1, s2, s3, s4 = lax.fori_loop(0, total, add_powers, (zero, zero, zero, zero))
    m = ((jnp.float32(total), s1, s2), (s1, s2, s3), (s2, s3, s4))

    def cross(p, q):
        return (p[1] * q[2] - p[2] * q[1], p[2] * q[0] - p[0] * q[2], p[0] * q[1] - p[1] * q[0])

    crosses = (cross(m[1], m[2]), cross(m[2], m[0]), cross(m[0], m[1]))
    det = m[0][0] * crosses[0][0] + m[0][1] * crosses[0][1] + m[0][2] * crosses[0][2]
    for t in range(3):
        for s in range(3):
            weight_s[2 * tiles + 3 * t + s] = crosses[s][t] / det
    for d in range(tiles):
        x = offset_of(member(d) * depth + k)
        weight_s[2 * d] = x
        weight_s[2 * d + 1] = x * x

    model[0] = jnp.zeros(model.shape[1:], jnp.float32)
    model[chunks + 1] = jnp.zeros(model.shape[1:], jnp.float32)

    loads[2].wait()
    def lag_of(hops):
        return HOP * hops

    lag_left = lag_of(k)
    lag_right = lag_of(depth - 1 - k)
    lag = jnp.maximum(lag_left, lag_right)

    def inside(j):
        return jnp.logical_and(j >= 0, j < chunks)

    half = (psf.shape[2] - 1) // 2
    wide = profile.shape[1]

    def step(s, carry):
        @pl.when(s < chunks)
        def _():
            j = s
            own = res[0, own_rows(a), columns(j)]
            sums = [own, own * weight_s[0], own * weight_s[1]]
            for d in range(1, tiles):
                raw_copy(j, d).wait_recv()
            for d in range(1, tiles):
                e = tiles - d
                piece = raw[j, d - 1]
                sums[0] += piece
                sums[1] += piece * weight_s[2 * e]
                sums[2] += piece * weight_s[2 * e + 1]
            for t in range(3):
                part[j, t] = sums[t]

        jl = s - lag_left

        @pl.when(inside(jl))
        def _():
            @pl.when(k == 0)
            def _():
                left_sum[jl] = part[jl]

            @pl.when(k > 0)
            def _():
                right_copy(jl).wait_recv()
                left_sum[jl] = left_in[jl] + part[jl]

            @pl.when(k < depth - 1)
            def _():
                right_copy(jl).start()

        jr = s - lag_right

        @pl.when(inside(jr))
        def _():
            @pl.when(k == depth - 1)
            def _():
                right_sum[jr] = part[jr]

            @pl.when(k < depth - 1)
            def _():
                left_copy(jr).wait_recv()
                right_sum[jr] = right_in[jr] + part[jr]

            @pl.when(k > 0)
            def _():
                left_copy(jr).start()

        jt = s - lag

        @pl.when(inside(jt))
        def _():
            @pl.when(k == 0)
            def _():
                steps[jt] = right_sum[jt]

            @pl.when(k > 0)
            def _():
                steps[jt] = left_in[jt] + right_sum[jt]

            g = [steps[jt, t] for t in range(3)]
            base = 2 * tiles
            u = [
                weight_s[base + 3 * t] * g[0]
                + weight_s[base + 3 * t + 1] * g[1]
                + weight_s[base + 3 * t + 2] * g[2]
                for t in range(3)
            ]
            for t in range(3):
                steps[jt, t] = u[t]
            for d in range(1, tiles):
                outgoing[jt, d - 1] = u[0] + weight_s[2 * d] * u[1] + weight_s[2 * d + 1] * u[2]
                model_copy(jt, d).start()
            model[jt + 1, own_rows(a)] = u[0] + weight_s[0] * u[1] + weight_s[1] * u[2]

        @pl.when(s == 1)
        def _():
            loads[1].wait()
            profile[...] = jnp.zeros_like(profile)
            profile[:, 0 : psf.shape[2]] = psf[0]
            band = pltpu.roll(
                jnp.broadcast_to(profile[1:2, :], (CHUNK, wide)), 0, 1, stride=1, stride_axis=0
            )
            row_high[...], row_low[...] = split_halves(band)
            band = pltpu.roll(
                jnp.broadcast_to(profile[0:1, :], (height, wide)), wide - half, 1, stride=1, stride_axis=0
            )[:, :height]
            col_high[...], col_low[...] = split_halves(band)

        jb = jt - BACK

        @pl.when(jnp.logical_and(jb + 1 >= 0, jb + 1 < chunks))
        def _():
            for d in range(1, tiles):
                model_copy(jb + 1, d).wait_recv()

        @pl.when(inside(jb))
        def _():
            field = jnp.concatenate(
                [model[jb, :, CHUNK - half :], model[jb + 1], model[jb + 2, :, :half]], axis=1
            )
            rowwise = dot_split(split_halves(field), (row_high[...], row_low[...]), ((1,), (1,)))
            blurred = dot_split((col_high[...], col_low[...]), split_halves(rowwise), ((1,), (0,)))
            result[jb] = res[0, :, columns(jb)] - blurred
            out_copy(jb).start()

        return carry

    lax.fori_loop(0, chunks + lag_of(depth - 1) + BACK, step, 0)

    per = taylor_out.shape[2] // CHUNK
    saves = [
        pltpu.make_async_copy(
            steps.at[k * per + i], taylor_out.at[:, :, pl.ds(i * CHUNK, CHUNK)], step_sem.at[i]
        )
        for i in range(per)
    ]
    for save in saves:
        save.start()

    def drain(j, carry):
        out_copy(j).wait()
        for d in range(1, tiles):
            raw_copy(j, d).wait_send()
            model_copy(j, d).wait_send()

        @pl.when(k < depth - 1)
        def _():
            right_copy(j).wait_send()

        @pl.when(k > 0)
        def _():
            left_copy(j).wait_send()

        return carry

    lax.fori_loop(0, chunks, drain, 0)
    for save in saves:
        save.wait()


def solution(mesh):
    tiles, depth = mesh.shape["tile"], mesh.shape["chan"]

    def shards(residual, freq_index, psf_profile):
        _, height, width = residual.shape
        rows, block = height // tiles, width // depth
        chunks = width // CHUNK
        half = (psf_profile.shape[2] - 1) // 2
        f32, bf16 = jnp.float32, jnp.bfloat16
        chain = pltpu.VMEM((chunks, 3, rows, CHUNK), f32)
        anywhere = pl.BlockSpec(memory_space=pltpu.HBM)
        dma = pltpu.SemaphoreType.DMA
        return pl.pallas_call(
            functools.partial(kernel, tiles, depth, chunks),
            out_shape=(
                jax.ShapeDtypeStruct((3, rows, block), f32),
                jax.ShapeDtypeStruct(residual.shape, f32),
            ),
            in_specs=[anywhere] * 3,
            out_specs=(anywhere, anywhere),
            scratch_shapes=[
                pltpu.VMEM(residual.shape, f32),
                pltpu.SMEM(freq_index.shape, jnp.int32),
                pltpu.VMEM(psf_profile.shape, f32),
                pltpu.VMEM((chunks, height, CHUNK), f32),
                pltpu.VMEM((chunks, tiles - 1, rows, CHUNK), f32),
                chain, chain, chain, chain, chain, chain,
                pltpu.VMEM((chunks, tiles - 1, rows, CHUNK), f32),
                pltpu.VMEM((chunks + 2, height, CHUNK), f32),
                pltpu.VMEM((2, CHUNK + 2 * half), f32),
                pltpu.VMEM((CHUNK, CHUNK + 2 * half), bf16),
                pltpu.VMEM((CHUNK, CHUNK + 2 * half), bf16),
                pltpu.VMEM((height, height), bf16),
                pltpu.VMEM((height, height), bf16),
                pltpu.SMEM((2 * tiles + 9,), f32),
                dma((chunks, tiles - 1)), dma((chunks, tiles - 1)),
                dma((chunks, tiles - 1)), dma((chunks, tiles - 1)),
                dma((chunks,)), dma((chunks,)), dma((chunks,)), dma((chunks,)),
                dma((3,)), dma((chunks,)), dma((block // CHUNK,)),
            ],
            compiler_params=pltpu.CompilerParams(
                collective_id=0, has_side_effects=True, vmem_limit_bytes=40 * 1024 * 1024
            ),
        )(residual, freq_index, psf_profile)

    in_specs = (
        P(("win", "tile", "chan"), None, None),
        P("win"),
        P(("win", "tile", "chan"), None, None),
    )
    out_specs = (P(None, ("win", "tile"), "chan"), P(("win", "tile", "chan"), None, None))
    return jax.shard_map(shards, mesh=mesh, in_specs=in_specs, out_specs=out_specs, check_vma=False)
```

```python
import functools

import jax
import jax.numpy as jnp
from jax import lax
from jax.experimental import pallas as pl
from jax.experimental.pallas import tpu as pltpu
from jax.sharding import PartitionSpec as P

FREQS = 1024
MESH = pl.DeviceIdType.MESH
HOP = 4
BACK = 6
CHUNK = 128
BLOCK = 2 * CHUNK


def split_halves(x):
    high = x.astype(jnp.bfloat16)
    low = (x - high.astype(jnp.float32)).astype(jnp.bfloat16)
    return high, low


def dot_split(a, b, dims):
    def one(x, y):
        return lax.dot_general(x, y, (dims, ((), ())), preferred_element_type=jnp.float32)

    return one(a[0], b[0]) + (one(a[0], b[1]) + one(a[1], b[0]))


def kernel(
    tiles, depth, chunks, res_hbm, freq_hbm, psf_hbm, taylor_out, new_out,
    res, freq, psf, result,
    raw, part, left_in, right_in, left_sum, right_sum, steps, outgoing, model,
    profile, row_high, row_low, col_high, col_low, weight_s,
    raw_send, raw_recv, mod_send, mod_recv, rt_send, rt_recv, lf_send, lf_recv,
    local, out_sem, step_sem,
):
    a = lax.axis_index("tile")
    k = lax.axis_index("chan")
    height = res.shape[1]
    rows = height // tiles
    total = freq.shape[0]

    loads = [
        pltpu.make_async_copy(freq_hbm, freq, local.at[0]),
        pltpu.make_async_copy(psf_hbm, psf, local.at[1]),
        pltpu.make_async_copy(res_hbm, res, local.at[2]),
    ]
    for load in loads:
        load.start()

    def member(d):
        return lax.rem(a + d, tiles)

    barrier = pltpu.get_barrier_semaphore()
    for d in range(1, tiles):
        pl.semaphore_signal(barrier, inc=1, device_id={"tile": member(d)}, device_id_type=MESH)

    @pl.when(k > 0)
    def _():
        pl.semaphore_signal(barrier, inc=1, device_id={"chan": k - 1}, device_id_type=MESH)

    @pl.when(k < depth - 1)
    def _():
        pl.semaphore_signal(barrier, inc=1, device_id={"chan": k + 1}, device_id_type=MESH)

    ends = jnp.where(k > 0, 1, 0) + jnp.where(k < depth - 1, 1, 0)
    pl.semaphore_wait(barrier, tiles - 1 + ends)

    def own_rows(b):
        return pl.ds(pl.multiple_of(b * rows, rows), rows)

    def columns(j):
        return pl.ds(pl.multiple_of(j * CHUNK, CHUNK), CHUNK)

    def raw_copy(j, d):
        return pltpu.make_async_remote_copy(
            src_ref=res_hbm.at[0, own_rows(member(d)), columns(j)],
            dst_ref=raw.at[j, d - 1],
            send_sem=raw_send.at[j, d - 1],
            recv_sem=raw_recv.at[j, d - 1],
            device_id={"tile": member(d)},
            device_id_type=MESH,
        )

    def model_copy(j, d):
        return pltpu.make_async_remote_copy(
            src_ref=outgoing.at[j, d - 1],
            dst_ref=model.at[j + 1, own_rows(a)],
            send_sem=mod_send.at[j, d - 1],
            recv_sem=mod_recv.at[j, d - 1],
            device_id={"tile": member(d)},
            device_id_type=MESH,
        )

    def right_copy(j):
        return pltpu.make_async_remote_copy(
            src_ref=left_sum.at[j], dst_ref=left_in.at[j],
            send_sem=rt_send.at[j], recv_sem=rt_recv.at[j],
            device_id={"chan": lax.rem(k + 1, depth)}, device_id_type=MESH,
        )

    def left_copy(j):
        return pltpu.make_async_remote_copy(
            src_ref=right_sum.at[j], dst_ref=right_in.at[j],
            send_sem=lf_send.at[j], recv_sem=lf_recv.at[j],
            device_id={"chan": lax.rem(k + depth - 1, depth)}, device_id_type=MESH,
        )

    def pair_columns(j):
        return pl.ds(pl.multiple_of(j * BLOCK, BLOCK), BLOCK)

    def out_copy(j):
        return pltpu.make_async_copy(
            result.at[j], new_out.at[0, :, pair_columns(j)], out_sem.at[j]
        )

    def send_raw(j, carry):
        for d in range(1, tiles):
            raw_copy(j, d).start()
        return carry

    lax.fori_loop(0, chunks, send_raw, 0)

    def offset_of(c):
        return 2.0 * freq[c].astype(jnp.float32) / (FREQS - 1) - 1.0

    def add_powers(c, sums):
        x = offset_of(c)
        y = x * x
        return sums[0] + x, sums[1] + y, sums[2] + x * y, sums[3] + y * y

    loads[0].wait()
    zero = jnp.float32(0.0)
    s1, s2, s3, s4 = lax.fori_loop(0, total, add_powers, (zero, zero, zero, zero))
    m = ((jnp.float32(total), s1, s2), (s1, s2, s3), (s2, s3, s4))

    def cross(p, q):
        return (p[1] * q[2] - p[2] * q[1], p[2] * q[0] - p[0] * q[2], p[0] * q[1] - p[1] * q[0])

    crosses = (cross(m[1], m[2]), cross(m[2], m[0]), cross(m[0], m[1]))
    det = m[0][0] * crosses[0][0] + m[0][1] * crosses[0][1] + m[0][2] * crosses[0][2]
    for t in range(3):
        for s in range(3):
            weight_s[2 * tiles + 3 * t + s] = crosses[s][t] / det
    for d in range(tiles):
        x = offset_of(member(d) * depth + k)
        weight_s[2 * d] = x
        weight_s[2 * d + 1] = x * x

    model[0] = jnp.zeros(model.shape[1:], jnp.float32)
    model[chunks + 1] = jnp.zeros(model.shape[1:], jnp.float32)

    loads[2].wait()
    def lag_of(hops):
        return HOP * hops

    lag_left = lag_of(k)
    lag_right = lag_of(depth - 1 - k)
    lag = jnp.maximum(lag_left, lag_right)

    def inside(j):
        return jnp.logical_and(j >= 0, j < chunks)

    half = (psf.shape[2] - 1) // 2
    wide = profile.shape[1]

    def step(s, carry):
        @pl.when(s < chunks)
        def _():
            j = s
            own = res[0, own_rows(a), columns(j)]
            sums = [own, own * weight_s[0], own * weight_s[1]]
            for d in range(1, tiles):
                raw_copy(j, d).wait_recv()
            for d in range(1, tiles):
                e = tiles - d
                piece = raw[j, d - 1]
                sums[0] += piece
                sums[1] += piece * weight_s[2 * e]
                sums[2] += piece * weight_s[2 * e + 1]
            for t in range(3):
                part[j, t] = sums[t]

        jl = s - lag_left

        @pl.when(inside(jl))
        def _():
            @pl.when(k == 0)
            def _():
                left_sum[jl] = part[jl]

            @pl.when(k > 0)
            def _():
                right_copy(jl).wait_recv()
                left_sum[jl] = left_in[jl] + part[jl]

            @pl.when(k < depth - 1)
            def _():
                right_copy(jl).start()

        jr = s - lag_right

        @pl.when(inside(jr))
        def _():
            @pl.when(k == depth - 1)
            def _():
                right_sum[jr] = part[jr]

            @pl.when(k < depth - 1)
            def _():
                left_copy(jr).wait_recv()
                right_sum[jr] = right_in[jr] + part[jr]

            @pl.when(k > 0)
            def _():
                left_copy(jr).start()

        jt = s - lag

        @pl.when(inside(jt))
        def _():
            @pl.when(k == 0)
            def _():
                steps[jt] = right_sum[jt]

            @pl.when(k > 0)
            def _():
                steps[jt] = left_in[jt] + right_sum[jt]

            g = [steps[jt, t] for t in range(3)]
            base = 2 * tiles
            u = [
                weight_s[base + 3 * t] * g[0]
                + weight_s[base + 3 * t + 1] * g[1]
                + weight_s[base + 3 * t + 2] * g[2]
                for t in range(3)
            ]
            for t in range(3):
                steps[jt, t] = u[t]
            for d in range(1, tiles):
                outgoing[jt, d - 1] = u[0] + weight_s[2 * d] * u[1] + weight_s[2 * d + 1] * u[2]
                model_copy(jt, d).start()
            model[jt + 1, own_rows(a)] = u[0] + weight_s[0] * u[1] + weight_s[1] * u[2]

        @pl.when(s == 1)
        def _():
            loads[1].wait()
            profile[...] = jnp.zeros_like(profile)
            profile[:, 0 : psf.shape[2]] = psf[0]
            band = pltpu.roll(
                jnp.broadcast_to(profile[1:2, :], (BLOCK, wide)), 0, 1, stride=1, stride_axis=0
            )
            row_high[...], row_low[...] = split_halves(band)
            band = pltpu.roll(
                jnp.broadcast_to(profile[0:1, :], (height, wide)), wide - half, 1, stride=1, stride_axis=0
            )[:, :height]
            col_high[...], col_low[...] = split_halves(band)

        jb = jt - BACK

        @pl.when(jnp.logical_and(jb + 1 >= 0, jb + 1 < chunks))
        def _():
            for d in range(1, tiles):
                model_copy(jb + 1, d).wait_recv()

        @pl.when(jnp.logical_and(inside(jb), lax.rem(jb + 2 * chunks, 2) == 1))
        def _():
            field = jnp.concatenate(
                [model[jb - 1, :, CHUNK - half :], model[jb], model[jb + 1], model[jb + 2, :, :half]],
                axis=1,
            )
            rowwise = dot_split(split_halves(field), (row_high[...], row_low[...]), ((1,), (1,)))
            blurred = dot_split((col_high[...], col_low[...]), split_halves(rowwise), ((1,), (0,)))
            pair = jb // 2
            result[pair] = res[0, :, pair_columns(pair)] - blurred
            out_copy(pair).start()

        return carry

    lax.fori_loop(0, chunks + lag_of(depth - 1) + BACK, step, 0)

    per = taylor_out.shape[2] // CHUNK
    saves = [
        pltpu.make_async_copy(
            steps.at[k * per + i], taylor_out.at[:, :, pl.ds(i * CHUNK, CHUNK)], step_sem.at[i]
        )
        for i in range(per)
    ]
    for save in saves:
        save.start()

    def drain(j, carry):
        for d in range(1, tiles):
            raw_copy(j, d).wait_send()
            model_copy(j, d).wait_send()

        @pl.when(k < depth - 1)
        def _():
            right_copy(j).wait_send()

        @pl.when(k > 0)
        def _():
            left_copy(j).wait_send()

        return carry

    lax.fori_loop(0, chunks, drain, 0)
    for i in range(chunks // 2):
        out_copy(i).wait()
    for save in saves:
        save.wait()


def solution(mesh):
    tiles, depth = mesh.shape["tile"], mesh.shape["chan"]

    def shards(residual, freq_index, psf_profile):
        _, height, width = residual.shape
        rows, block = height // tiles, width // depth
        chunks = width // CHUNK
        half = (psf_profile.shape[2] - 1) // 2
        f32, bf16 = jnp.float32, jnp.bfloat16
        chain = pltpu.VMEM((chunks, 3, rows, CHUNK), f32)
        anywhere = pl.BlockSpec(memory_space=pltpu.HBM)
        dma = pltpu.SemaphoreType.DMA
        return pl.pallas_call(
            functools.partial(kernel, tiles, depth, chunks),
            out_shape=(
                jax.ShapeDtypeStruct((3, rows, block), f32),
                jax.ShapeDtypeStruct(residual.shape, f32),
            ),
            in_specs=[anywhere] * 3,
            out_specs=(anywhere, anywhere),
            scratch_shapes=[
                pltpu.VMEM(residual.shape, f32),
                pltpu.SMEM(freq_index.shape, jnp.int32),
                pltpu.VMEM(psf_profile.shape, f32),
                pltpu.VMEM((chunks // 2, height, BLOCK), f32),
                pltpu.VMEM((chunks, tiles - 1, rows, CHUNK), f32),
                chain, chain, chain, chain, chain, chain,
                pltpu.VMEM((chunks, tiles - 1, rows, CHUNK), f32),
                pltpu.VMEM((chunks + 2, height, CHUNK), f32),
                pltpu.VMEM((2, BLOCK + 2 * half), f32),
                pltpu.VMEM((BLOCK, BLOCK + 2 * half), bf16),
                pltpu.VMEM((BLOCK, BLOCK + 2 * half), bf16),
                pltpu.VMEM((height, height), bf16),
                pltpu.VMEM((height, height), bf16),
                pltpu.SMEM((2 * tiles + 9,), f32),
                dma((chunks, tiles - 1)), dma((chunks, tiles - 1)),
                dma((chunks, tiles - 1)), dma((chunks, tiles - 1)),
                dma((chunks,)), dma((chunks,)), dma((chunks,)), dma((chunks,)),
                dma((3,)), dma((chunks // 2,)), dma((block // CHUNK,)),
            ],
            compiler_params=pltpu.CompilerParams(
                collective_id=0, has_side_effects=True, vmem_limit_bytes=40 * 1024 * 1024
            ),
        )(residual, freq_index, psf_profile)

    in_specs = (
        P(("win", "tile", "chan"), None, None),
        P("win"),
        P(("win", "tile", "chan"), None, None),
    )
    out_specs = (P(None, ("win", "tile"), "chan"), P(("win", "tile", "chan"), None, None))
    return jax.shard_map(shards, mesh=mesh, in_specs=in_specs, out_specs=out_specs, check_vma=False)
```

```python
import functools

import jax
import jax.numpy as jnp
from jax import lax
from jax.experimental import pallas as pl
from jax.experimental.pallas import tpu as pltpu
from jax.sharding import PartitionSpec as P

FREQS = 1024
MESH = pl.DeviceIdType.MESH
HOP = 4
BACK = 6
CHUNK = 128
BLOCK = 2 * CHUNK


def split_halves(x):
    high = x.astype(jnp.bfloat16)
    low = (x - high.astype(jnp.float32)).astype(jnp.bfloat16)
    return high, low


def dot_split(a, b, dims):
    def one(x, y):
        return lax.dot_general(x, y, (dims, ((), ())), preferred_element_type=jnp.float32)

    return one(a[0], b[0]) + (one(a[0], b[1]) + one(a[1], b[0]))


def kernel(
    tiles, depth, chunks, res_hbm, freq_hbm, psf_hbm, taylor_out, new_out,
    res, freq, psf, result,
    raw, part, left_in, right_in, left_sum, right_sum, steps, outgoing, model,
    profile, row_high, row_low, col_high, col_low, weight_s,
    raw_send, raw_recv, mod_send, mod_recv, rt_send, rt_recv, lf_send, lf_recv,
    local, out_sem, step_sem,
):
    a = lax.axis_index("tile")
    k = lax.axis_index("chan")
    height = res.shape[1]
    rows = height // tiles
    total = freq.shape[0]

    loads = [
        pltpu.make_async_copy(freq_hbm, freq, local.at[0]),
        pltpu.make_async_copy(psf_hbm, psf, local.at[1]),
        pltpu.make_async_copy(res_hbm, res, local.at[2]),
    ]
    for load in loads:
        load.start()

    def member(d):
        return lax.rem(a + d, tiles)

    barrier = pltpu.get_barrier_semaphore()
    for d in range(1, tiles):
        pl.semaphore_signal(barrier, inc=1, device_id={"tile": member(d)}, device_id_type=MESH)

    @pl.when(k > 0)
    def _():
        pl.semaphore_signal(barrier, inc=1, device_id={"chan": k - 1}, device_id_type=MESH)

    @pl.when(k < depth - 1)
    def _():
        pl.semaphore_signal(barrier, inc=1, device_id={"chan": k + 1}, device_id_type=MESH)

    ends = jnp.where(k > 0, 1, 0) + jnp.where(k < depth - 1, 1, 0)
    pl.semaphore_wait(barrier, tiles - 1 + ends)

    def own_rows(b):
        return pl.ds(pl.multiple_of(b * rows, rows), rows)

    def columns(j):
        return pl.ds(pl.multiple_of(j * CHUNK, CHUNK), CHUNK)

    def raw_copy(j, d):
        return pltpu.make_async_remote_copy(
            src_ref=res_hbm.at[0, own_rows(member(d)), columns(j)],
            dst_ref=raw.at[j, d - 1],
            send_sem=raw_send.at[j, d - 1],
            recv_sem=raw_recv.at[j, d - 1],
            device_id={"tile": member(d)},
            device_id_type=MESH,
        )

    def model_copy(j, d):
        return pltpu.make_async_remote_copy(
            src_ref=outgoing.at[j, d - 1],
            dst_ref=model.at[j + 1, own_rows(a)],
            send_sem=mod_send.at[j, d - 1],
            recv_sem=mod_recv.at[j, d - 1],
            device_id={"tile": member(d)},
            device_id_type=MESH,
        )

    def right_copy(j):
        return pltpu.make_async_remote_copy(
            src_ref=left_sum.at[j], dst_ref=left_in.at[j],
            send_sem=rt_send.at[j], recv_sem=rt_recv.at[j],
            device_id={"chan": lax.rem(k + 1, depth)}, device_id_type=MESH,
        )

    def left_copy(j):
        return pltpu.make_async_remote_copy(
            src_ref=right_sum.at[j], dst_ref=right_in.at[j],
            send_sem=lf_send.at[j], recv_sem=lf_recv.at[j],
            device_id={"chan": lax.rem(k + depth - 1, depth)}, device_id_type=MESH,
        )

    def pair_columns(j):
        return pl.ds(pl.multiple_of(j * BLOCK, BLOCK), BLOCK)

    def out_copy(j):
        return pltpu.make_async_copy(
            result.at[j], new_out.at[0, :, pair_columns(j)], out_sem.at[j]
        )

    def send_raw(j, carry):
        for d in (*range(2, tiles), 1):
            raw_copy(j, d).start()
        return carry

    lax.fori_loop(0, chunks, send_raw, 0)

    def offset_of(c):
        return 2.0 * freq[c].astype(jnp.float32) / (FREQS - 1) - 1.0

    def add_powers(c, sums):
        x = offset_of(c)
        y = x * x
        return sums[0] + x, sums[1] + y, sums[2] + x * y, sums[3] + y * y

    loads[0].wait()
    zero = jnp.float32(0.0)
    s1, s2, s3, s4 = lax.fori_loop(0, total, add_powers, (zero, zero, zero, zero))
    m = ((jnp.float32(total), s1, s2), (s1, s2, s3), (s2, s3, s4))

    def cross(p, q):
        return (p[1] * q[2] - p[2] * q[1], p[2] * q[0] - p[0] * q[2], p[0] * q[1] - p[1] * q[0])

    crosses = (cross(m[1], m[2]), cross(m[2], m[0]), cross(m[0], m[1]))
    det = m[0][0] * crosses[0][0] + m[0][1] * crosses[0][1] + m[0][2] * crosses[0][2]
    for t in range(3):
        for s in range(3):
            weight_s[2 * tiles + 3 * t + s] = crosses[s][t] / det
    for d in range(tiles):
        x = offset_of(member(d) * depth + k)
        weight_s[2 * d] = x
        weight_s[2 * d + 1] = x * x

    model[0] = jnp.zeros(model.shape[1:], jnp.float32)
    model[chunks + 1] = jnp.zeros(model.shape[1:], jnp.float32)

    loads[2].wait()
    def lag_of(hops):
        return HOP * hops

    lag_left = lag_of(k)
    lag_right = lag_of(depth - 1 - k)
    lag = jnp.maximum(lag_left, lag_right)

    def inside(j):
        return jnp.logical_and(j >= 0, j < chunks)

    half = (psf.shape[2] - 1) // 2
    wide = profile.shape[1]

    def step(s, carry):
        @pl.when(s < chunks)
        def _():
            j = s
            own = res[0, own_rows(a), columns(j)]
            sums = [own, own * weight_s[0], own * weight_s[1]]
            for d in range(1, tiles):
                raw_copy(j, d).wait_recv()
            for d in range(1, tiles):
                e = tiles - d
                piece = raw[j, d - 1]
                sums[0] += piece
                sums[1] += piece * weight_s[2 * e]
                sums[2] += piece * weight_s[2 * e + 1]
            for t in range(3):
                part[j, t] = sums[t]

        jl = s - lag_left

        @pl.when(inside(jl))
        def _():
            @pl.when(k == 0)
            def _():
                left_sum[jl] = part[jl]

            @pl.when(k > 0)
            def _():
                right_copy(jl).wait_recv()
                left_sum[jl] = left_in[jl] + part[jl]

            @pl.when(k < depth - 1)
            def _():
                right_copy(jl).start()

        jr = s - lag_right

        @pl.when(inside(jr))
        def _():
            @pl.when(k == depth - 1)
            def _():
                right_sum[jr] = part[jr]

            @pl.when(k < depth - 1)
            def _():
                left_copy(jr).wait_recv()
                right_sum[jr] = right_in[jr] + part[jr]

            @pl.when(k > 0)
            def _():
                left_copy(jr).start()

        jt = s - lag

        @pl.when(inside(jt))
        def _():
            @pl.when(k == 0)
            def _():
                steps[jt] = right_sum[jt]

            @pl.when(k > 0)
            def _():
                steps[jt] = left_in[jt] + right_sum[jt]

            g = [steps[jt, t] for t in range(3)]
            base = 2 * tiles
            u = [
                weight_s[base + 3 * t] * g[0]
                + weight_s[base + 3 * t + 1] * g[1]
                + weight_s[base + 3 * t + 2] * g[2]
                for t in range(3)
            ]
            for t in range(3):
                steps[jt, t] = u[t]
            for d in (*range(2, tiles), 1):
                outgoing[jt, d - 1] = u[0] + weight_s[2 * d] * u[1] + weight_s[2 * d + 1] * u[2]
                model_copy(jt, d).start()
            model[jt + 1, own_rows(a)] = u[0] + weight_s[0] * u[1] + weight_s[1] * u[2]

        @pl.when(s == 1)
        def _():
            loads[1].wait()
            profile[...] = jnp.zeros_like(profile)
            profile[:, 0 : psf.shape[2]] = psf[0]
            band = pltpu.roll(
                jnp.broadcast_to(profile[1:2, :], (BLOCK, wide)), 0, 1, stride=1, stride_axis=0
            )
            row_high[...], row_low[...] = split_halves(band)
            band = pltpu.roll(
                jnp.broadcast_to(profile[0:1, :], (height, wide)), wide - half, 1, stride=1, stride_axis=0
            )[:, :height]
            col_high[...], col_low[...] = split_halves(band)

        jb = jt - BACK

        @pl.when(jnp.logical_and(jb + 1 >= 0, jb + 1 < chunks))
        def _():
            for d in range(1, tiles):
                model_copy(jb + 1, d).wait_recv()

        @pl.when(jnp.logical_and(inside(jb), lax.rem(jb + 2 * chunks, 2) == 1))
        def _():
            field = jnp.concatenate(
                [model[jb - 1, :, CHUNK - half :], model[jb], model[jb + 1], model[jb + 2, :, :half]],
                axis=1,
            )
            rowwise = dot_split(split_halves(field), (row_high[...], row_low[...]), ((1,), (1,)))
            blurred = dot_split((col_high[...], col_low[...]), split_halves(rowwise), ((1,), (0,)))
            pair = jb // 2
            result[pair] = res[0, :, pair_columns(pair)] - blurred
            out_copy(pair).start()

        return carry

    lax.fori_loop(0, chunks + lag_of(depth - 1) + BACK, step, 0)

    per = taylor_out.shape[2] // CHUNK
    saves = [
        pltpu.make_async_copy(
            steps.at[k * per + i], taylor_out.at[:, :, pl.ds(i * CHUNK, CHUNK)], step_sem.at[i]
        )
        for i in range(per)
    ]
    for save in saves:
        save.start()

    def drain(j, carry):
        for d in range(1, tiles):
            raw_copy(j, d).wait_send()
            model_copy(j, d).wait_send()

        @pl.when(k < depth - 1)
        def _():
            right_copy(j).wait_send()

        @pl.when(k > 0)
        def _():
            left_copy(j).wait_send()

        return carry

    lax.fori_loop(0, chunks, drain, 0)
    for i in range(chunks // 2):
        out_copy(i).wait()
    for save in saves:
        save.wait()


def solution(mesh):
    tiles, depth = mesh.shape["tile"], mesh.shape["chan"]

    def shards(residual, freq_index, psf_profile):
        _, height, width = residual.shape
        rows, block = height // tiles, width // depth
        chunks = width // CHUNK
        half = (psf_profile.shape[2] - 1) // 2
        f32, bf16 = jnp.float32, jnp.bfloat16
        chain = pltpu.VMEM((chunks, 3, rows, CHUNK), f32)
        anywhere = pl.BlockSpec(memory_space=pltpu.HBM)
        dma = pltpu.SemaphoreType.DMA
        return pl.pallas_call(
            functools.partial(kernel, tiles, depth, chunks),
            out_shape=(
                jax.ShapeDtypeStruct((3, rows, block), f32),
                jax.ShapeDtypeStruct(residual.shape, f32),
            ),
            in_specs=[anywhere] * 3,
            out_specs=(anywhere, anywhere),
            scratch_shapes=[
                pltpu.VMEM(residual.shape, f32),
                pltpu.SMEM(freq_index.shape, jnp.int32),
                pltpu.VMEM(psf_profile.shape, f32),
                pltpu.VMEM((chunks // 2, height, BLOCK), f32),
                pltpu.VMEM((chunks, tiles - 1, rows, CHUNK), f32),
                chain, chain, chain, chain, chain, chain,
                pltpu.VMEM((chunks, tiles - 1, rows, CHUNK), f32),
                pltpu.VMEM((chunks + 2, height, CHUNK), f32),
                pltpu.VMEM((2, BLOCK + 2 * half), f32),
                pltpu.VMEM((BLOCK, BLOCK + 2 * half), bf16),
                pltpu.VMEM((BLOCK, BLOCK + 2 * half), bf16),
                pltpu.VMEM((height, height), bf16),
                pltpu.VMEM((height, height), bf16),
                pltpu.SMEM((2 * tiles + 9,), f32),
                dma((chunks, tiles - 1)), dma((chunks, tiles - 1)),
                dma((chunks, tiles - 1)), dma((chunks, tiles - 1)),
                dma((chunks,)), dma((chunks,)), dma((chunks,)), dma((chunks,)),
                dma((3,)), dma((chunks // 2,)), dma((block // CHUNK,)),
            ],
            compiler_params=pltpu.CompilerParams(
                collective_id=0, has_side_effects=True, vmem_limit_bytes=40 * 1024 * 1024
            ),
        )(residual, freq_index, psf_profile)

    in_specs = (
        P(("win", "tile", "chan"), None, None),
        P("win"),
        P(("win", "tile", "chan"), None, None),
    )
    out_specs = (P(None, ("win", "tile"), "chan"), P(("win", "tile", "chan"), None, None))
    return jax.shard_map(shards, mesh=mesh, in_specs=in_specs, out_specs=out_specs, check_vma=False)
```
